32 devices in a mesh: pipe: 2 (over core), tensor: 4 (over y, x), dp: 4 (over z).
Axes of the slice: x: 2, y: 2, z: 4, core: 2. Of those that a mesh axis runs over, the one named last changes fastest.
Arguments:
- tokens: bfloat16 [4096, 768], P('dp'), may hold values from -6 to 6
- cotangent: bfloat16 [4096, 768], P('dp'), may hold values from -6 to 6
- ln_gain: float32 [2, 2, 768], P('pipe'), may hold values from 0.5 to 1.5
- ln_bias: float32 [2, 2, 768], P('pipe'), may hold values from -3 to 3
- w_qkv: bfloat16 [2, 3, 768, 768], P('pipe', None, None, 'tensor'), may hold values from -0.21875 to 0.21875
- b_qv: float32 [2, 2, 768], P('pipe', None, 'tensor'), may hold values from -3 to 3
- w_out: bfloat16 [2, 768, 768], P('pipe', 'tensor'), may hold values from -1.25 to 1.25
- b_out: float32 [2, 768], P('pipe'), may hold values from -3 to 3
- w_fc: bfloat16 [2, 768, 3072], P('pipe', None, 'tensor'), may hold values from -0.21875 to 0.21875
- b_fc: float32 [2, 3072], P('pipe', 'tensor'), may hold values from -3 to 3
- w_proj: bfloat16 [2, 3072, 768], P('pipe', 'tensor'), may hold values from -0.109375 to 0.109375
- b_proj: float32 [2, 768], P('pipe'), may hold values from -3 to 3
Outputs:
- activations: bfloat16 [2, 4096, 768], P('pipe', 'dp')
- grad_inputs: float32 [2, 4096, 768], P('pipe', 'dp')
- grad_ln_gain: float32 [2, 2, 768], P('pipe')
- grad_ln_bias: float32 [2, 2, 768], P('pipe')
- grad_qkv: float32 [2, 3, 768, 768], P('pipe', None, None, 'tensor')
- grad_b_qv: float32 [2, 2, 768], P('pipe', None, 'tensor')
- grad_out: float32 [2, 768, 768], P('pipe', 'tensor')
- grad_b_out: float32 [2, 768], P('pipe')
- grad_fc: float32 [2, 768, 3072], P('pipe', None, 'tensor')
- grad_b_fc: float32 [2, 3072], P('pipe', 'tensor')
- grad_proj: float32 [2, 3072, 768], P('pipe', 'tensor')
- grad_b_proj: float32 [2, 768], P('pipe')
The draws below stay inside these ranges and needn't reach their ends.
All inputs are finite; a program needn't handle non-finite values.
Results may differ from the reference program's by a relative error of at most 0.013.
Values may be sent and summed in bfloat16 or wider, within the bound.
No kernel may reach another device: no remote copies, remote signals or barrier semaphores. Data moves between devices by JAX's collectives and lax.ppermute only.
A program may use at most 128 MiB of HBM per device.

```python
import jax
import jax.numpy as jnp
from jax import lax

D = 768
HEADS = 12
HEAD_DIM = 64
FF = 3072
LENGTH = 1024
HD = 768
TOKENS = 4096


def block_scale(rng, extent, split, smallest, largest):
    factor_of, own = 1.0, jax.random.fold_in(rng, 6)
    for axis_at, shards_of in split:
        steps = jnp.exp(jax.random.uniform(jax.random.fold_in(own, axis_at), (shards_of,), jnp.float32, smallest / len(split), largest / len(split)))
        factor_of = factor_of * jnp.repeat(steps, extent[axis_at] // shards_of).reshape([-1 if axis == axis_at else 1 for axis in range(len(extent))])
    return factor_of


def scatter_about(own_key, extent, scale, bound, shards=(), kind=jnp.bfloat16):
    array = scale * jax.random.normal(own_key, extent, jnp.float32)
    if shards:
        array = array * block_scale(own_key, extent, shards, -0.22, 0.18)
    return jnp.clip(array, -bound, bound).astype(kind)


def setup_inputs(seed: int = 0) -> dict:
    arg_keys = jax.random.split(jax.random.key(seed), 13)
    tokens = scatter_about(arg_keys[0], (TOKENS, D), 1.0, 6.0, ((0, 4),))
    cotangent = scatter_about(arg_keys[1], (TOKENS, D), 1.0, 6.0, ((0, 4),))
    ln_gain = jnp.clip(1.0 + 0.1 * jax.random.normal(arg_keys[2], (2, 2, D), jnp.float32), 0.5, 1.5)
    ln_bias = scatter_about(arg_keys[3], (2, 2, D), 0.3, 3.0, ((0, 2),), jnp.float32)
    w_qkv = scatter_about(arg_keys[4], (2, 3, D, HD), D ** -0.5, 0.21875, ((0, 2), (3, 4)))
    b_qv = scatter_about(arg_keys[5], (2, 2, HD), 0.3, 3.0, ((0, 2), (2, 4)), jnp.float32)
    w_out = scatter_about(arg_keys[6], (2, HD, D), (D // 32) ** -0.5, 1.25, ((0, 2), (1, 4)))
    b_out = scatter_about(arg_keys[7], (2, D), 0.3, 3.0, ((0, 2),), jnp.float32)
    w_fc = scatter_about(arg_keys[8], (2, D, FF), D ** -0.5, 0.21875, ((0, 2), (2, 4)))
    b_fc = scatter_about(arg_keys[9], (2, FF), 0.3, 3.0, ((0, 2), (1, 4)), jnp.float32)
    w_proj = scatter_about(arg_keys[10], (2, FF, D), FF ** -0.5, 0.109375, ((0, 2), (1, 4)))
    b_proj = scatter_about(arg_keys[11], (2, D), 0.3, 3.0, ((0, 2),), jnp.float32)
    return dict(tokens=tokens, cotangent=cotangent, ln_gain=ln_gain, ln_bias=ln_bias, w_qkv=w_qkv, b_qv=b_qv, w_out=w_out, b_out=b_out, w_fc=w_fc, b_fc=b_fc, w_proj=w_proj, b_proj=b_proj)


@jax.custom_vjp
def low(v):
    return lax.optimization_barrier(v.astype(jnp.bfloat16)).astype(jnp.float32)

@jax.custom_vjp
def low_back(v):
    return v

def low_keep(v):
    return (low(v), None)

def low_pass(kept, grad):
    return (grad,)

def back_keep(v):
    return (v, None)

def back_low(kept, grad):
    return (low(grad),)
low.defvjp(low_keep, low_pass)
low_back.defvjp(back_keep, back_low)
EPSILON = 1e-05
PRECISE = lax.Precision.HIGHEST

def matmul(left, right):
    return jnp.dot(left, right, precision=PRECISE, preferred_element_type=jnp.float32)

def layer_norm(inputs, scale_vec, shift_vec):
    centred = inputs - lax.optimization_barrier(jnp.mean(inputs, axis=-1, keepdims=True))
    spread = lax.optimization_barrier(jnp.mean(centred * centred, axis=-1, keepdims=True))
    return centred * lax.rsqrt(spread + EPSILON) * scale_vec + shift_vec

def block_sequence(params, inflow):
    ln_gain, ln_bias, w_qkv, b_qv, w_out, b_out, w_fc, b_fc, w_proj, b_proj = params
    seq_len = inflow.shape[0]
    normed = low(layer_norm(inflow, ln_gain[0], ln_bias[0]))
    queries = low(low_back(matmul(normed, w_qkv[0])) + b_qv[0]).reshape(seq_len, HEADS, HEAD_DIM)
    key_rows = low(low_back(matmul(normed, w_qkv[1]))).reshape(seq_len, HEADS, HEAD_DIM)
    values = low(low_back(matmul(normed, w_qkv[2])) + b_qv[1]).reshape(seq_len, HEADS, HEAD_DIM)
    scores = low_back(jnp.einsum('qhd,khd->hqk', queries, key_rows, precision=PRECISE) * HEAD_DIM ** (-0.5))
    positions = jnp.arange(seq_len)
    allowed = positions[None, :] <= positions[:, None]
    scores = jnp.where(allowed[None], scores, -1e+30)
    row_top = lax.optimization_barrier(jnp.max(scores, axis=-1, keepdims=True))
    exp_scores = jnp.exp(scores - row_top)
    weights = low(exp_scores / lax.optimization_barrier(jnp.sum(exp_scores, axis=-1, keepdims=True)))
    mixed_heads = jnp.einsum('hqk,khd->qhd', weights, values, precision=PRECISE).reshape(seq_len, HEADS * HEAD_DIM)
    mixed_heads = low(low_back(mixed_heads))
    hidden = inflow + low_back(matmul(mixed_heads, w_out)) + b_out
    normed_two = low(layer_norm(hidden, ln_gain[1], ln_bias[1]))
    pre_act = low_back(matmul(normed_two, w_fc)) + b_fc
    gelu_out = low(jax.nn.gelu(pre_act, approximate=True))
    return hidden + low_back(matmul(gelu_out, w_proj)) + b_proj

def block_all(params, inflow):
    sequences = inflow.reshape(-1, LENGTH, D)
    per_sequence = jax.checkpoint(lambda piece: block_sequence(params, piece))
    return lax.map(per_sequence, sequences).reshape(inflow.shape)

def reference(tokens, cotangent, ln_gain, ln_bias, w_qkv, b_qv, w_out, b_out, w_fc, b_fc, w_proj, b_proj):
    stacked = [source.astype(jnp.float32) for source in (ln_gain, ln_bias, w_qkv, b_qv, w_out, b_out, w_fc, b_fc, w_proj, b_proj)]
    first = tuple((source[0] for source in stacked))
    second = tuple((source[1] for source in stacked))
    out_one, back_one = jax.vjp(block_all, first, tokens.astype(jnp.float32))
    sent = low(out_one)
    out_two, back_two = jax.vjp(block_all, second, sent)
    grads_two, grad_sent = back_two(cotangent.astype(jnp.float32))
    grads_one, grad_tokens = back_one(low(grad_sent))
    merged = [jnp.stack([first_grad, second_grad]) for first_grad, second_grad in zip(grads_one, grads_two)]
    activations = jnp.stack([sent, out_two]).astype(jnp.bfloat16)
    grad_inputs = jnp.stack([grad_tokens, grad_sent])
    return (activations, grad_inputs, merged[0], merged[1], merged[2], merged[3], merged[4], merged[5], merged[6], merged[7], merged[8], merged[9])
```

```python
import jax
import jax.numpy as jnp
from jax import lax
from jax.sharding import PartitionSpec as P

HEAD_DIM = 64
LENGTH = 1024
EPSILON = 1e-05
SCALE = HEAD_DIM ** (-0.5)
BF = jnp.bfloat16
F32 = jnp.float32


def swap(value, axis, mask):
    count = lax.axis_size(axis)
    return lax.ppermute(value, axis, [(i, i ^ mask) for i in range(count)])


def layer_norm(inputs, scale_vec, shift_vec):
    centred = inputs - jnp.mean(inputs, axis=-1, keepdims=True)
    spread = jnp.mean(centred * centred, axis=-1, keepdims=True)
    return centred * lax.rsqrt(spread + EPSILON) * scale_vec + shift_vec


def gelu_tanh(inputs):
    return jax.nn.gelu(inputs, approximate=True)


def mm(left, right):
    return jnp.dot(left, right, preferred_element_type=F32)


def rows_dot(left, right):
    return lax.dot_general(left, right, (((0,), (0,)), ((), ())), preferred_element_type=F32)


def back_dot(left, right):
    return lax.dot_general(left, right, (((1,), (1,)), ((), ())), preferred_element_type=F32)


def spread_rows(share):
    return [share] + [swap(share, "tensor", m) for m in range(1, lax.axis_size("tensor"))]


def sum_rows(pieces):
    total = pieces[0].astype(F32)
    for m in range(1, len(pieces)):
        total = total + swap(pieces[m].astype(BF), "tensor", m).astype(F32)
    return total


def local(
    tokens, cotangent, ln_gain, ln_bias, w_qkv, b_qv, w_out, b_out, w_fc, b_fc, w_proj, b_proj
):
    core = lax.axis_index("pipe")
    place = lax.axis_index("tensor")
    line = lax.axis_index("dp")
    parts = lax.axis_size("tensor")
    dp_count = lax.axis_size("dp")
    total_rows, width = tokens.shape
    seqs = total_rows // LENGTH
    half = LENGTH // 2
    rows = seqs * half
    share = rows // parts
    piece_rows = half // parts
    inner = w_qkv.shape[3]
    heads = inner // HEAD_DIM
    hidden = w_fc.shape[2]
    first_core = core == 0

    def both(value):
        other = swap(value, "pipe", 1)
        return jnp.where(first_core, value, other), jnp.where(first_core, other, value)

    def relative(whole):
        stack = whole.reshape(seqs, 2, parts, piece_rows, width)
        mine = lax.dynamic_index_in_dim(stack, core, 1, False)
        return [
            lax.dynamic_index_in_dim(mine, place ^ m, 1, False).reshape(share, width)
            for m in range(parts)
        ]

    def natural(pieces, dtype):
        out = jnp.zeros((seqs, parts, piece_rows, width), dtype)
        for m in range(parts):
            out = lax.dynamic_update_index_in_dim(
                out, pieces[m].astype(dtype).reshape(seqs, piece_rows, width), place ^ m, 1
            )
        return out

    vec_parts = [ln_gain[0].reshape(-1), ln_bias[0].reshape(-1), b_qv[0].reshape(-1), b_out[0], b_fc[0], b_proj[0]]
    sizes = [v.shape[0] for v in vec_parts]
    vec_both = both(jnp.concatenate(vec_parts))
    qkv_both = both(w_qkv[0])
    out_both = both(w_out[0])
    fc_both = both(w_fc[0])
    proj_both = both(w_proj[0])

    piece_index = jnp.arange(half) // piece_rows
    places = (place ^ piece_index) * piece_rows + jnp.arange(half) % piece_rows
    query_places = core * half + places
    key_places = jnp.concatenate([query_places, (1 - core) * half + places])
    allowed = (key_places[None, :] <= query_places[:, None])[None, None]

    def to_heads(value, length):
        if seqs > 1:
            value = value.reshape(parts, seqs, piece_rows, -1).transpose(1, 0, 2, 3)
        return value.reshape(seqs, length, heads, HEAD_DIM)

    def from_heads(value):
        value = value.reshape(seqs, half, inner)
        if seqs > 1:
            value = value.reshape(seqs, parts, piece_rows, inner).transpose(1, 0, 2, 3)
        return value.reshape(rows, inner)

    def split_vec(vec):
        out, at = [], 0
        for size in sizes:
            out.append(vec[at : at + size])
            at += size
        gain, shift, qv, mix, up, down = out
        return gain.reshape(2, width), shift.reshape(2, width), qv.reshape(2, inner), mix, up, down

    def cut(value):
        return [value[m * share : (m + 1) * share] for m in range(parts)]

    def forward(block, pieces):
        gain, shift, qv, mix_bias, up_bias, down_bias = split_vec(vec_both[block])
        w_three, w_mix, w_up, w_down = qkv_both[block], out_both[block], fc_both[block], proj_both[block]
        inflow = jnp.concatenate(pieces).astype(F32)
        normed = layer_norm(inflow, gain[0], shift[0]).astype(BF)
        query = (mm(normed, w_three[0]) + qv[0]).astype(BF)
        key = mm(normed, w_three[1]).astype(BF)
        value = (mm(normed, w_three[2]) + qv[1]).astype(BF)
        pair = jnp.concatenate([key, value], axis=1)
        pair_other = swap(pair, "pipe", 1)
        key_heads = jnp.concatenate(
            [to_heads(key, half), to_heads(pair_other[:, :inner], half)], axis=1
        )
        value_heads = jnp.concatenate(
            [to_heads(value, half), to_heads(pair_other[:, inner:], half)], axis=1
        )
        query_heads = to_heads(query, half)
        scores = (
            jnp.einsum("sqhd,skhd->shqk", query_heads, key_heads, preferred_element_type=F32) * SCALE
        )
        scores = jnp.where(allowed, scores, -1e30)
        top = jnp.max(scores, axis=-1, keepdims=True)
        exps = jnp.exp(scores - top)
        total = jnp.sum(exps, axis=-1, keepdims=True)
        probs = (exps / total).astype(BF)
        mixed = from_heads(
            jnp.einsum("shqk,skhd->sqhd", probs, value_heads, preferred_element_type=F32)
        ).astype(BF)
        log_total = top + jnp.log(total)
        mix_part = mm(mixed, w_mix)
        residual = pieces[0].astype(F32) + sum_rows(cut(mix_part)) + mix_bias
        normed_two = spread_rows(layer_norm(residual, gain[1], shift[1]).astype(BF))
        normed_two = jnp.concatenate(normed_two)
        pre_act = mm(normed_two, w_up) + up_bias
        gelu_out = gelu_tanh(pre_act).astype(BF)
        down_part = mm(gelu_out, w_down)
        result = residual + sum_rows(cut(down_part)) + down_bias
        out_pieces = spread_rows(result.astype(BF))
        kept = dict(
            pieces=pieces, normed=normed, query=query_heads, key=key_heads, value=value_heads,
            mixed=mixed, log_total=log_total, residual=residual, normed_two=normed_two,
            pre_act=pre_act, gelu_out=gelu_out,
        )
        return out_pieces, kept

    def backward(block, kept, grad_pieces):
        gain, shift, qv, mix_bias, up_bias, down_bias = split_vec(vec_both[block])
        w_three, w_mix, w_up, w_down = qkv_both[block], out_both[block], fc_both[block], proj_both[block]
        grad_result = jnp.concatenate(grad_pieces)
        grad_share = grad_pieces[0].astype(F32)
        grad_gelu = back_dot(grad_result, w_down)
        _, gelu_back = jax.vjp(gelu_tanh, kept["pre_act"])
        grad_pre = gelu_back(grad_gelu)[0]
        pre_bf = grad_pre.astype(BF)
        up_part = back_dot(pre_bf, w_up)
        _, norm_two_back = jax.vjp(layer_norm, kept["residual"], gain[1], shift[1])
        grad_norm, g_gain_two, g_shift_two = norm_two_back(sum_rows(cut(up_part)))
        grad_hidden = grad_share + grad_norm
        hidden_bf = jnp.concatenate(spread_rows(grad_hidden.astype(BF)))
        g_down = reduce_grad(rows_dot(kept["gelu_out"], grad_result))
        g_up = reduce_grad(rows_dot(kept["normed_two"], pre_bf))
        g_mix = reduce_grad(rows_dot(kept["mixed"], hidden_bf))
        grad_mixed = to_heads(back_dot(hidden_bf, w_mix).astype(BF), half)
        query_heads, key_heads, value_heads = kept["query"], kept["key"], kept["value"]
        scores = (
            jnp.einsum("sqhd,skhd->shqk", query_heads, key_heads, preferred_element_type=F32) * SCALE
        )
        probs = jnp.where(allowed, jnp.exp(scores - kept["log_total"]), 0.0)
        grad_probs = jnp.einsum(
            "sqhd,skhd->shqk", grad_mixed, value_heads, preferred_element_type=F32
        )
        value_grad = jnp.einsum(
            "shqk,sqhd->skhd", probs.astype(BF), grad_mixed, preferred_element_type=F32
        )
        delta = jnp.sum(probs * grad_probs, axis=-1, keepdims=True)
        grad_raw = (probs * (grad_probs - delta)).astype(BF)
        grad_query = (
            from_heads(
                jnp.einsum("shqk,skhd->sqhd", grad_raw, key_heads, preferred_element_type=F32)
            )
            * SCALE
        )
        key_grad = (
            jnp.einsum("shqk,sqhd->skhd", grad_raw, query_heads, preferred_element_type=F32) * SCALE
        )
        away = swap(
            jnp.concatenate(
                [from_heads(key_grad[:, half:]), from_heads(value_grad[:, half:])], axis=1
            ).astype(BF),
            "pipe",
            1,
        ).astype(F32)
        key_total = from_heads(key_grad[:, :half]) + away[:, :inner]
        value_total = from_heads(value_grad[:, :half]) + away[:, inner:]
        three_bf = jnp.concatenate([grad_query, key_total, value_total], axis=1).astype(BF)
        w_flat = jnp.concatenate([w_three[0], w_three[1], w_three[2]], axis=1)
        normed_part = back_dot(three_bf, w_flat)
        own_rows = kept["pieces"][0].astype(F32)
        _, norm_one_back = jax.vjp(layer_norm, own_rows, gain[0], shift[0])
        g_three = reduce_grad(rows_dot(kept["normed"], three_bf))
        grad_norm_one, g_gain_one, g_shift_one = norm_one_back(sum_rows(cut(normed_part)))
        grad_inflow = grad_hidden + grad_norm_one
        grad_in_pieces = spread_rows(grad_inflow.astype(BF))
        shared = jnp.stack(
            [g_gain_one, g_gain_two, g_shift_one, g_shift_two]
            + [jnp.sum(grad_hidden, axis=0), jnp.sum(grad_share, axis=0)]
        )
        private = jnp.concatenate(
            [jnp.sum(grad_query, axis=0), jnp.sum(value_total, axis=0), jnp.sum(grad_pre, axis=0)]
        )
        return grad_in_pieces, (g_down, g_up, g_mix, g_three), shared, private

    at_end = (line == 0) | (line == dp_count - 1)

    def line_sum(value):
        if dp_count != 4:
            return lax.psum(value, "dp")
        inward = lax.ppermute(value, "dp", [(0, 1), (3, 2)])
        pair = value + inward
        across = lax.ppermute(pair, "dp", [(1, 2), (2, 1)])
        total = pair + across
        outward = lax.ppermute(total, "dp", [(1, 0), (2, 3)])
        return jnp.where(at_end, outward, total)

    def reduce_grad(grad):
        size = grad.shape[0] // 2
        mine = lax.dynamic_slice_in_dim(grad, core * size, size, 0)
        theirs = lax.dynamic_slice_in_dim(grad, (1 - core) * size, size, 0)
        got = swap(theirs.astype(BF), "pipe", 1)
        return line_sum((mine + got.astype(F32)).astype(BF))

    def join_halves(zero, one):
        from_one = lax.ppermute(zero, "pipe", [(1, 0)])
        from_zero = lax.ppermute(one, "pipe", [(0, 1)])
        low = jnp.where(first_core, zero, from_zero)
        high = jnp.where(first_core, from_one, one)
        return jnp.concatenate([low, high]).astype(F32)

    def join_rows(zero, one, dtype):
        zero_nat, one_nat = natural(zero, BF), natural(one, BF)
        from_one = lax.ppermute(zero_nat, "pipe", [(1, 0)])
        from_zero = lax.ppermute(one_nat, "pipe", [(0, 1)])
        low = jnp.where(first_core, zero_nat, from_zero)
        high = jnp.where(first_core, from_one, one_nat)
        whole = jnp.stack([low, high], axis=1)
        return whole.reshape(total_rows, width).astype(dtype)

    def small_sum(value):
        total = value
        if dp_count == 4:
            total = total + swap(total, "pipe", 1)
            return sum([swap(total, "dp", m) for m in range(1, 4)], total)
        return lax.psum(total, ("pipe", "dp"))

    def group_sum(value):
        return sum([swap(value, "tensor", m) for m in range(1, parts)], value)

    zero_out, zero_kept = forward(0, relative(tokens))
    one_out, one_kept = forward(1, zero_out)
    one_grad, one_big, one_shared, one_private = backward(1, one_kept, relative(cotangent))
    zero_grad, zero_big, zero_shared, zero_private = backward(0, zero_kept, one_grad)

    activations = join_rows(zero_out, one_out, BF)
    grad_inputs = join_rows(zero_grad, one_grad, F32)
    g_down, g_up, g_mix, g_three = [join_halves(z, o) for z, o in zip(zero_big, one_big)]
    shared = [small_sum(group_sum(v)) for v in (zero_shared, one_shared)]
    private = [small_sum(v) for v in (zero_private, one_private)]
    shared = jnp.where(first_core, shared[0], shared[1])
    private = jnp.where(first_core, private[0], private[1])
    g_three = g_three.reshape(width, 3, inner).transpose(1, 0, 2)
    return (
        activations[None],
        grad_inputs[None],
        shared[None, 0:2],
        shared[None, 2:4],
        g_three[None],
        private[: 2 * inner].reshape(1, 2, inner),
        g_mix[None],
        shared[None, 4],
        g_up[None],
        private[None, 2 * inner :],
        g_down[None],
        shared[None, 5],
    )


def solution(mesh):
    in_specs = (
        P("dp", None),
        P("dp", None),
        P("pipe", None, None),
        P("pipe", None, None),
        P("pipe", None, None, "tensor"),
        P("pipe", None, "tensor"),
        P("pipe", "tensor", None),
        P("pipe", None),
        P("pipe", None, "tensor"),
        P("pipe", "tensor"),
        P("pipe", "tensor", None),
        P("pipe", None),
    )
    out_specs = (
        P("pipe", "dp", None),
        P("pipe", "dp", None),
        P("pipe", None, None),
        P("pipe", None, None),
        P("pipe", None, None, "tensor"),
        P("pipe", None, "tensor"),
        P("pipe", "tensor", None),
        P("pipe", None),
        P("pipe", None, "tensor"),
        P("pipe", "tensor"),
        P("pipe", "tensor", None),
        P("pipe", None),
    )
    return jax.shard_map(local, mesh=mesh, in_specs=in_specs, out_specs=out_specs, check_vma=False)
```

```python
import jax
import jax.numpy as jnp
from jax import lax
from jax.sharding import PartitionSpec as P

HEAD_DIM = 64
LENGTH = 1024
EPSILON = 1e-05
SCALE = HEAD_DIM ** (-0.5)
BF = jnp.bfloat16
F32 = jnp.float32


def swap(value, axis, mask):
    count = lax.axis_size(axis)
    return lax.ppermute(value, axis, [(i, i ^ mask) for i in range(count)])


def layer_norm(inputs, scale_vec, shift_vec):
    centred = inputs - jnp.mean(inputs, axis=-1, keepdims=True)
    spread = jnp.mean(centred * centred, axis=-1, keepdims=True)
    return centred * lax.rsqrt(spread + EPSILON) * scale_vec + shift_vec


def gelu_tanh(inputs):
    return jax.nn.gelu(inputs, approximate=True)


def mm(left, right):
    return jnp.dot(left, right, preferred_element_type=F32)


def rows_dot(left, right):
    return lax.dot_general(left, right, (((0,), (0,)), ((), ())), preferred_element_type=F32)


def back_dot(left, right):
    return lax.dot_general(left, right, (((1,), (1,)), ((), ())), preferred_element_type=F32)


def spread_rows(share):
    return [share] + [swap(share, "tensor", m) for m in range(1, lax.axis_size("tensor"))]


def sum_rows(pieces):
    total = pieces[0].astype(F32)
    for m in range(1, len(pieces)):
        total = total + swap(pieces[m].astype(BF), "tensor", m).astype(F32)
    return total


def local(
    tokens, cotangent, ln_gain, ln_bias, w_qkv, b_qv, w_out, b_out, w_fc, b_fc, w_proj, b_proj
):
    core = lax.axis_index("pipe")
    place = lax.axis_index("tensor")
    line = lax.axis_index("dp")
    parts = lax.axis_size("tensor")
    dp_count = lax.axis_size("dp")
    total_rows, width = tokens.shape
    seqs = total_rows // LENGTH
    half = LENGTH // 2
    rows = seqs * half
    share = rows // parts
    piece_rows = half // parts
    inner = w_qkv.shape[3]
    heads = inner // HEAD_DIM
    hidden = w_fc.shape[2]
    first_core = core == 0

    def both(value):
        other = swap(value, "pipe", 1)
        return jnp.where(first_core, value, other), jnp.where(first_core, other, value)

    def relative(whole):
        stack = whole.reshape(seqs, 2, parts, piece_rows, width)
        mine = lax.dynamic_index_in_dim(stack, core, 1, False)
        return [
            lax.dynamic_index_in_dim(mine, place ^ m, 1, False).reshape(share, width)
            for m in range(parts)
        ]

    def widen(vec):
        return jnp.pad(vec, ((0, 0), (0, width - vec.shape[1]))) if vec.shape[1] < width else vec

    up_rows = -(-hidden // width)
    vec_rows = jnp.concatenate(
        [ln_gain[0], ln_bias[0], b_out, b_proj, b_fc.reshape(up_rows, -1), widen(b_qv[0])], axis=0
    )
    vec_both = both(vec_rows)
    qkv_both = both(w_qkv[0])
    out_both = both(w_out[0])
    fc_both = both(w_fc[0])
    proj_both = both(w_proj[0])

    piece_index = jnp.arange(half) // piece_rows
    places = (place ^ piece_index) * piece_rows + jnp.arange(half) % piece_rows
    query_places = core * half + places
    key_places = jnp.concatenate([query_places, (1 - core) * half + places])
    allowed = (key_places[None, :] <= query_places[:, None])[None, None]

    def to_heads(value, length):
        if seqs > 1:
            value = value.reshape(parts, seqs, piece_rows, -1).transpose(1, 0, 2, 3)
        return value.reshape(seqs, length, heads, HEAD_DIM)

    def from_heads(value):
        value = value.reshape(seqs, half, inner)
        if seqs > 1:
            value = value.reshape(seqs, parts, piece_rows, inner).transpose(1, 0, 2, 3)
        return value.reshape(rows, inner)

    def split_vec(vec):
        down_at = 6 + up_rows
        qv = vec[down_at : down_at + 2, :inner]
        return vec[0:2], vec[2:4], qv, vec[4], vec[6:down_at].reshape(hidden), vec[5]

    def cut(value):
        return [value[m * share : (m + 1) * share] for m in range(parts)]

    def forward(block, pieces):
        gain, shift, qv, mix_bias, up_bias, down_bias = split_vec(vec_both[block])
        w_three, w_mix, w_up, w_down = qkv_both[block], out_both[block], fc_both[block], proj_both[block]
        inflow = jnp.concatenate(pieces).astype(F32)
        normed = layer_norm(inflow, gain[0], shift[0]).astype(BF)
        query = (mm(normed, w_three[0]) + qv[0]).astype(BF)
        key = mm(normed, w_three[1]).astype(BF)
        value = (mm(normed, w_three[2]) + qv[1]).astype(BF)
        pair = jnp.concatenate([key, value], axis=1)
        pair_other = swap(pair, "pipe", 1)
        key_heads = jnp.concatenate(
            [to_heads(key, half), to_heads(pair_other[:, :inner], half)], axis=1
        )
        value_heads = jnp.concatenate(
            [to_heads(value, half), to_heads(pair_other[:, inner:], half)], axis=1
        )
        query_heads = to_heads(query, half)
        scores = (
            jnp.einsum("sqhd,skhd->shqk", query_heads, key_heads, preferred_element_type=F32) * SCALE
        )
        scores = jnp.where(allowed, scores, -1e30)
        top = jnp.max(scores, axis=-1, keepdims=True)
        exps = jnp.exp(scores - top)
        total = jnp.sum(exps, axis=-1, keepdims=True)
        probs = (exps / total).astype(BF)
        mixed = from_heads(
            jnp.einsum("shqk,skhd->sqhd", probs, value_heads, preferred_element_type=F32)
        ).astype(BF)
        log_total = top + jnp.log(total)
        mix_part = mm(mixed, w_mix)
        residual = pieces[0].astype(F32) + sum_rows(cut(mix_part)) + mix_bias
        normed_two = spread_rows(layer_norm(residual, gain[1], shift[1]).astype(BF))
        pre_act = [mm(piece, w_up) + up_bias for piece in normed_two]
        gelu_out = [gelu_tanh(piece).astype(BF) for piece in pre_act]
        down_part = [mm(piece, w_down) for piece in gelu_out]
        result = residual + sum_rows(down_part) + down_bias
        out_pieces = spread_rows(result.astype(BF))
        kept = dict(
            pieces=pieces, normed=normed, query=query_heads, key=key_heads, value=value_heads,
            mixed=mixed, log_total=log_total, residual=residual, normed_two=normed_two,
            pre_act=pre_act, gelu_out=gelu_out,
        )
        return out_pieces, kept

    def core_sum(left, right, axis):
        picked = left if axis == 0 else right
        size = picked.shape[1] // 2
        mine = lax.dynamic_slice_in_dim(picked, core * size, size, 1)
        theirs = lax.dynamic_slice_in_dim(picked, (1 - core) * size, size, 1)
        if axis == 0:
            sent = rows_dot(theirs, right).astype(BF)
            return (rows_dot(mine, right) + swap(sent, "pipe", 1).astype(F32)).astype(BF)
        sent = rows_dot(left, theirs).astype(BF)
        return (rows_dot(left, mine) + swap(sent, "pipe", 1).astype(F32)).astype(BF)

    def small_rows(values):
        stack = jnp.stack(values).astype(BF)
        return jnp.pad(stack, ((0, 16 - stack.shape[0]), (0, 0)))

    def backward(block, kept, grad_pieces):
        gain, shift, qv, mix_bias, up_bias, down_bias = split_vec(vec_both[block])
        w_three, w_mix, w_up, w_down = qkv_both[block], out_both[block], fc_both[block], proj_both[block]
        grad_share = grad_pieces[0].astype(F32)
        grad_pre = []
        for pre, piece in zip(kept["pre_act"], grad_pieces):
            grad_pre.append(jax.vjp(gelu_tanh, pre)[1](back_dot(piece, w_down))[0])
        pre_bf = [piece.astype(BF) for piece in grad_pre]
        up_part = [back_dot(piece, w_up) for piece in pre_bf]
        _, norm_two_back = jax.vjp(layer_norm, kept["residual"], gain[1], shift[1])
        grad_norm, g_gain_two, g_shift_two = norm_two_back(sum_rows(up_part))
        grad_hidden = grad_share + grad_norm
        hidden_bf = jnp.concatenate(spread_rows(grad_hidden.astype(BF)))
        g_down = core_sum(jnp.concatenate(kept["gelu_out"]), jnp.concatenate(grad_pieces), 0)
        g_up = core_sum(jnp.concatenate(kept["normed_two"]), jnp.concatenate(pre_bf), 0)
        g_mix = core_sum(kept["mixed"], hidden_bf, 1)
        grad_mixed = to_heads(back_dot(hidden_bf, w_mix).astype(BF), half)
        query_heads, key_heads, value_heads = kept["query"], kept["key"], kept["value"]
        scores = (
            jnp.einsum("sqhd,skhd->shqk", query_heads, key_heads, preferred_element_type=F32) * SCALE
        )
        probs = jnp.where(allowed, jnp.exp(scores - kept["log_total"]), 0.0)
        grad_probs = jnp.einsum(
            "sqhd,skhd->shqk", grad_mixed, value_heads, preferred_element_type=F32
        )
        value_grad = jnp.einsum(
            "shqk,sqhd->skhd", probs.astype(BF), grad_mixed, preferred_element_type=F32
        )
        delta = jnp.sum(probs * grad_probs, axis=-1, keepdims=True)
        grad_raw = (probs * (grad_probs - delta)).astype(BF)
        grad_query = (
            from_heads(
                jnp.einsum("shqk,skhd->sqhd", grad_raw, key_heads, preferred_element_type=F32)
            )
            * SCALE
        )
        key_grad = (
            jnp.einsum("shqk,sqhd->skhd", grad_raw, query_heads, preferred_element_type=F32) * SCALE
        )
        away = swap(
            jnp.concatenate(
                [from_heads(key_grad[:, half:]), from_heads(value_grad[:, half:])], axis=1
            ).astype(BF),
            "pipe",
            1,
        ).astype(F32)
        key_total = from_heads(key_grad[:, :half]) + away[:, :inner]
        value_total = from_heads(value_grad[:, :half]) + away[:, inner:]
        three_bf = jnp.concatenate([grad_query, key_total, value_total], axis=1).astype(BF)
        w_flat = jnp.concatenate([w_three[0], w_three[1], w_three[2]], axis=1)
        normed_part = back_dot(three_bf, w_flat)
        own_rows = kept["pieces"][0].astype(F32)
        _, norm_one_back = jax.vjp(layer_norm, own_rows, gain[0], shift[0])
        g_three = core_sum(kept["normed"], three_bf, 0)
        grad_norm_one, g_gain_one, g_shift_one = norm_one_back(sum_rows(cut(normed_part)))
        grad_inflow = grad_hidden + grad_norm_one
        riders = small_rows(
            [g_gain_one, g_gain_two, g_shift_one, g_shift_two]
            + [jnp.sum(grad_hidden, axis=0), jnp.sum(grad_share, axis=0)]
        )
        gathered = spread_rows(jnp.concatenate([grad_inflow.astype(BF), riders]))
        grad_in_pieces = [piece[:share] for piece in gathered]
        shared = sum([piece[share:].astype(F32) for piece in gathered[1:]], gathered[0][share:].astype(F32))
        private_up = sum([jnp.sum(piece, axis=0) for piece in grad_pre[1:]], jnp.sum(grad_pre[0], axis=0))
        private = jnp.concatenate(
            [
                shared[:6],
                private_up.reshape(up_rows, -1),
                widen(jnp.sum(grad_query, axis=0)[None]),
                widen(jnp.sum(value_total, axis=0)[None]),
            ]
        )
        private = jnp.pad(private, ((0, 16 - private.shape[0]), (0, 0)))
        return grad_in_pieces, g_down, g_up, g_mix, g_three, private

    def direct_sum(value):
        if dp_count != 4:
            return lax.psum(value, "dp")
        size = value.shape[0] // 4
        stack = value.reshape(4, size, value.shape[1])
        total = lax.dynamic_index_in_dim(stack, line, 0, False).astype(F32)
        for m in (1, 3, 2):
            piece = lax.dynamic_index_in_dim(stack, line ^ m, 0, False)
            total = total + swap(piece, "dp", m).astype(F32)
        total = total.astype(BF)
        got = jnp.stack([total] + [swap(total, "dp", m) for m in (1, 2, 3)])
        return jnp.concatenate(
            [lax.dynamic_index_in_dim(got, line ^ j, 0, False) for j in range(4)]
        )

    def swap_halves(zero, one):
        return swap(jnp.where(first_core, one, zero), "pipe", 1)

    def join_halves(zero, one, other, axis=0):
        low = jnp.where(first_core, zero, other)
        high = jnp.where(first_core, other, one)
        return jnp.concatenate([low, high], axis=axis).astype(F32)

    def natural(pieces):
        out = list(pieces)
        bit = 1
        while bit < parts:
            flip = (place & bit) != 0
            out = [jnp.where(flip, out[j ^ bit], out[j]) for j in range(parts)]
            bit *= 2
        return out

    def join_rows(zero, one, dtype):
        own = jnp.where(first_core, jnp.concatenate(zero), jnp.concatenate(one))
        got = swap(jnp.where(first_core, jnp.concatenate(one), jnp.concatenate(zero)), "pipe", 1)
        low = natural(cut(jnp.where(first_core, own, got)))
        high = natural(cut(jnp.where(first_core, got, own)))
        if seqs > 1:
            whole = jnp.stack([piece.reshape(seqs, piece_rows, width) for piece in low + high], axis=1)
        else:
            whole = jnp.concatenate(low + high)
        return whole.reshape(total_rows, width).astype(dtype)

    zero_out, zero_kept = forward(0, relative(tokens))
    one_out, one_kept = forward(1, zero_out)
    activations = join_rows(zero_out, one_out, BF)
    one_grad, one_down, one_up, one_mix, one_three, one_small = backward(
        1, one_kept, relative(cotangent)
    )
    first_sum = lax.psum(jnp.concatenate([one_down, one_up]), "dp")
    zero_grad, zero_down, zero_up, zero_mix, zero_three, zero_small = backward(
        0, zero_kept, one_grad
    )
    mixed_rows = inner // 2
    second = jnp.concatenate(
        [
            one_mix.reshape(mixed_rows, width),
            one_three.reshape(-1, width),
            one_small.astype(BF),
            zero_down,
            zero_up,
        ]
    )
    second, first_sum = lax.optimization_barrier((second, first_sum))
    second_sum = lax.psum(second, "dp")
    three_rows = one_three.size // width
    ends, at = [], 0
    for size in (mixed_rows, three_rows, 16, zero_down.shape[0], zero_up.shape[0]):
        ends.append(second_sum[at : at + size])
        at += size
    one_mix, one_three, one_small = ends[0].reshape(one_mix.shape), ends[1].reshape(one_three.shape), ends[2]
    zero_down, zero_up = ends[3], ends[4]
    one_down, one_up = first_sum[: zero_down.shape[0]], first_sum[zero_down.shape[0] :]
    zero_three = direct_sum(zero_three)
    zero_mix = direct_sum(zero_mix)
    grad_inputs = join_rows(zero_grad, one_grad, F32)
    g_down = join_halves(zero_down, one_down, swap_halves(zero_down, one_down))
    g_up = join_halves(zero_up, one_up, swap_halves(zero_up, one_up))
    g_mix = join_halves(zero_mix, one_mix, swap_halves(zero_mix, one_mix), 1)
    g_three = join_halves(zero_three, one_three, swap_halves(zero_three, one_three))
    if dp_count == 4:
        zero_small = sum([swap(zero_small, "dp", m) for m in (1, 2, 3)], zero_small)
    else:
        zero_small = lax.psum(zero_small, "dp")
    one_small = one_small.astype(F32)
    small = jnp.where(first_core, zero_small, one_small) + swap_halves(zero_small, one_small)
    g_three = g_three.reshape(width, 3, inner).transpose(1, 0, 2)
    qv_at = 6 + up_rows
    return (
        activations[None],
        grad_inputs[None],
        small[None, 0:2],
        small[None, 2:4],
        g_three[None],
        small[None, qv_at : qv_at + 2, :inner],
        g_mix[None],
        small[None, 4],
        g_up[None],
        small[6:qv_at].reshape(1, hidden),
        g_down[None],
        small[None, 5],
    )


def solution(mesh):
    in_specs = (
        P("dp", None),
        P("dp", None),
        P("pipe", None, None),
        P("pipe", None, None),
        P("pipe", None, None, "tensor"),
        P("pipe", None, "tensor"),
        P("pipe", "tensor", None),
        P("pipe", None),
        P("pipe", None, "tensor"),
        P("pipe", "tensor"),
        P("pipe", "tensor", None),
        P("pipe", None),
    )
    out_specs = (
        P("pipe", "dp", None),
        P("pipe", "dp", None),
        P("pipe", None, None),
        P("pipe", None, None),
        P("pipe", None, None, "tensor"),
        P("pipe", None, "tensor"),
        P("pipe", "tensor", None),
        P("pipe", None),
        P("pipe", None, "tensor"),
        P("pipe", "tensor"),
        P("pipe", "tensor", None),
        P("pipe", None),
    )
    return jax.shard_map(local, mesh=mesh, in_specs=in_specs, out_specs=out_specs, check_vma=False)
```

```python
import jax
import jax.numpy as jnp
from jax import lax
from jax.experimental import pallas as pl
from jax.experimental.pallas import tpu as pltpu
from jax.sharding import PartitionSpec as P

HEAD_DIM = 64
LENGTH = 1024
EPSILON = 1e-05
SCALE = HEAD_DIM ** (-0.5)
BF = jnp.bfloat16
F32 = jnp.float32


def swap(value, axis, mask):
    count = lax.axis_size(axis)
    return lax.ppermute(value, axis, [(i, i ^ mask) for i in range(count)])


def layer_norm(inputs, scale_vec, shift_vec):
    centred = inputs - jnp.mean(inputs, axis=-1, keepdims=True)
    spread = jnp.mean(centred * centred, axis=-1, keepdims=True)
    return centred * lax.rsqrt(spread + EPSILON) * scale_vec + shift_vec


def gelu_tanh(inputs):
    return jax.nn.gelu(inputs, approximate=True)


def mm(left, right):
    return jnp.dot(left, right, preferred_element_type=F32)


def rows_dot(left, right):
    return lax.dot_general(left, right, (((0,), (0,)), ((), ())), preferred_element_type=F32)


def back_dot(left, right):
    return lax.dot_general(left, right, (((1,), (1,)), ((), ())), preferred_element_type=F32)


def spread_rows(share):
    return [share] + [swap(share, "tensor", m) for m in range(1, lax.axis_size("tensor"))]


def sum_rows(pieces):
    total = pieces[0].astype(F32)
    for m in range(1, len(pieces)):
        total = total + swap(pieces[m].astype(BF), "tensor", m).astype(F32)
    return total


def after(value, *earlier):
    return lax.optimization_barrier((value,) + earlier)[0]


def tie_kernel(*refs):
    del refs


def tie(value, *earlier):
    anywhere = pl.BlockSpec(memory_space=pl.ANY)
    return pl.pallas_call(
        tie_kernel,
        in_specs=[anywhere] * (1 + len(earlier)),
        out_specs=anywhere,
        out_shape=jax.ShapeDtypeStruct(value.shape, value.dtype),
        input_output_aliases={0: 0},
        name="tie",
    )(value, *earlier)


def nt_dot(left, right):
    return lax.dot_general(left, right, (((1,), (1,)), ((), ())), preferred_element_type=F32)


def key_bias(where_ref, rows):
    core, shift = where_ref[0], where_ref[1] * where_ref[2]
    keys = lax.broadcasted_iota(jnp.int32, (rows, rows), 0) ^ shift
    queries = lax.broadcasted_iota(jnp.int32, (rows, rows), 1) ^ shift
    own = jnp.where(keys <= queries, 0.0, -1e30)
    return own, jnp.where(core == 1, 0.0, -1e30)


def attend_kernel(where_ref, query_ref, own_ref, other_ref, mixed_ref, log_ref):
    rows, inner = query_ref.shape
    own_bias, other_bias = key_bias(where_ref, rows)
    own_value = own_ref[:, inner:].astype(F32).T.astype(BF)
    other_value = other_ref[:, inner:].astype(F32).T.astype(BF)
    mixed, logs = [], []
    for at in range(0, inner, HEAD_DIM):
        cols = slice(at, at + HEAD_DIM)
        query = query_ref[:, cols]
        own = nt_dot(own_ref[:, cols], query) * SCALE + own_bias
        other = nt_dot(other_ref[:, cols], query) * SCALE + other_bias
        top = jnp.maximum(
            jnp.max(own, axis=0, keepdims=True), jnp.max(other, axis=0, keepdims=True)
        )
        own, other = jnp.exp(own - top), jnp.exp(other - top)
        total = jnp.sum(own, axis=0, keepdims=True) + jnp.sum(other, axis=0, keepdims=True)
        scale = 1.0 / total
        mixed.append(
            mm(own_value[cols], (own * scale).astype(BF))
            + mm(other_value[cols], (other * scale).astype(BF))
        )
        logs.append(top + jnp.log(total))
    mixed_ref[...] = jnp.concatenate(mixed, axis=0).T.astype(BF)
    log_ref[...] = jnp.concatenate(logs, axis=0)


def attend_call(where, query, own, other):
    rows, inner = query.shape
    heads = inner // HEAD_DIM
    vmem = pl.BlockSpec(memory_space=pltpu.VMEM)
    return pl.pallas_call(
        attend_kernel,
        in_specs=[pl.BlockSpec(memory_space=pltpu.SMEM)] + [vmem] * 3,
        out_specs=[vmem] * 2,
        out_shape=[
            jax.ShapeDtypeStruct((rows, inner), BF),
            jax.ShapeDtypeStruct((heads, rows), F32),
        ],
        compiler_params=pltpu.CompilerParams(vmem_limit_bytes=40 * 2**20),
        cost_estimate=pl.CostEstimate(
            flops=8 * rows * rows * inner,
            bytes_accessed=rows * inner * 12,
            transcendentals=2 * rows * rows * heads,
        ),
        name="attend",
    )(where, query, own, other)


def attend_back_kernel(
    where_ref, query_ref, own_ref, other_ref, grad_ref, log_ref, query_out, own_out, other_out
):
    rows, inner = query_ref.shape
    own_bias, other_bias = key_bias(where_ref, rows)
    own_key = own_ref[:, :inner].astype(F32).T.astype(BF)
    other_key = other_ref[:, :inner].astype(F32).T.astype(BF)
    grad_query = []
    for head, at in enumerate(range(0, inner, HEAD_DIM)):
        cols = slice(at, at + HEAD_DIM)
        values = slice(inner + at, inner + at + HEAD_DIM)
        query, grad = query_ref[:, cols], grad_ref[:, cols]
        log_total = log_ref[head : head + 1, :]
        own = jnp.exp(nt_dot(own_ref[:, cols], query) * SCALE + own_bias - log_total)
        other = jnp.exp(nt_dot(other_ref[:, cols], query) * SCALE + other_bias - log_total)
        own_grad = nt_dot(own_ref[:, values], grad)
        other_grad = nt_dot(other_ref[:, values], grad)
        own_out[:, values] = mm(own.astype(BF), grad)
        other_out[:, values] = mm(other.astype(BF), grad).astype(BF)
        delta = jnp.sum(own * own_grad, axis=0, keepdims=True) + jnp.sum(
            other * other_grad, axis=0, keepdims=True
        )
        own_raw = (own * (own_grad - delta)).astype(BF)
        other_raw = (other * (other_grad - delta)).astype(BF)
        own_out[:, cols] = mm(own_raw, query) * SCALE
        other_out[:, cols] = (mm(other_raw, query) * SCALE).astype(BF)
        grad_query.append(mm(own_key[cols], own_raw) + mm(other_key[cols], other_raw))
    query_out[...] = jnp.concatenate(grad_query, axis=0).T * SCALE


def attend_back_call(where, query, own, other, grad, log_total):
    rows, inner = query.shape
    heads = inner // HEAD_DIM
    vmem = pl.BlockSpec(memory_space=pltpu.VMEM)
    return pl.pallas_call(
        attend_back_kernel,
        in_specs=[pl.BlockSpec(memory_space=pltpu.SMEM)] + [vmem] * 5,
        out_specs=[vmem] * 3,
        out_shape=[
            jax.ShapeDtypeStruct((rows, inner), F32),
            jax.ShapeDtypeStruct((rows, 2 * inner), F32),
            jax.ShapeDtypeStruct((rows, 2 * inner), BF),
        ],
        compiler_params=pltpu.CompilerParams(vmem_limit_bytes=40 * 2**20),
        cost_estimate=pl.CostEstimate(
            flops=20 * rows * rows * inner,
            bytes_accessed=rows * inner * 26,
            transcendentals=2 * rows * rows * heads,
        ),
        name="attend_back",
    )(where, query, own, other, grad, log_total)


def pick_source(where_ref, half, refs, put):
    core = where_ref[0]
    for at, ref in enumerate(refs):
        mine = (half == core) if at < 2 else (half != core)

        @pl.when(mine & (core == at % 2))
        def _(ref=ref):
            put(ref)


def source_used(where_ref, half, at):
    core = where_ref[0]
    return ((half == core) if at < 2 else (half != core)) & (core == at % 2)


def join_rows_kernel(where_ref, *refs):
    place, half = where_ref[1], pl.program_id(0)
    out_ref = refs[-1]
    size = refs[0].shape[0] // out_ref.shape[0]

    def put(ref):
        for j in range(out_ref.shape[0]):
            rows = pl.ds(pl.multiple_of((place ^ j) * size, size), size)
            out_ref[j] = ref[rows, :].astype(out_ref.dtype)

    pick_source(where_ref, half, refs[:4], put)


def join_rows_call(where, sources, parts, dtype):
    rows, width = sources[0].shape
    size = rows // parts
    out = pl.pallas_call(
        join_rows_kernel,
        grid_spec=pltpu.PrefetchScalarGridSpec(
            num_scalar_prefetch=1,
            grid=(2,),
            in_specs=[pl.BlockSpec((rows, width), lambda h, w: (0, 0))] * 4,
            out_specs=pl.BlockSpec((parts, size, width), lambda h, w: (h, 0, 0)),
        ),
        out_shape=jax.ShapeDtypeStruct((2 * parts, size, width), dtype),
        compiler_params=pltpu.CompilerParams(vmem_limit_bytes=32 * 2**20),
        cost_estimate=pl.CostEstimate(flops=0, bytes_accessed=rows * width * 12, transcendentals=0),
        name="join_rows",
    )(where, *sources)
    return out.reshape(2 * rows, width)


def join_ffn_kernel(where_ref, *refs):
    which, half = pl.program_id(0), pl.program_id(1)
    down_ref, up_ref = refs[-2:]

    def put(ref):
        @pl.when(which == 0)
        def _():
            down_ref[...] = ref[...].astype(F32)

        @pl.when(which == 1)
        def _():
            up_ref[...] = ref[...].astype(F32)

    pick_source(where_ref, half, refs[:4], put)


def join_ffn_call(where, sources, rows, width):
    def source(at):
        return pl.BlockSpec(
            (rows, width), lambda k, h, w: (jnp.where(source_used(w, h, at) | (h == 1), k, 0), 0)
        )

    shape = jax.ShapeDtypeStruct((2 * rows, width), F32)
    return pl.pallas_call(
        join_ffn_kernel,
        grid_spec=pltpu.PrefetchScalarGridSpec(
            num_scalar_prefetch=1,
            grid=(2, 2),
            in_specs=[source(at) for at in range(4)],
            out_specs=[
                pl.BlockSpec((rows, width), lambda k, h, w: (jnp.where(k == 0, h, 1), 0)),
                pl.BlockSpec((rows, width), lambda k, h, w: (jnp.where(k == 0, 0, h), 0)),
            ],
        ),
        out_shape=[shape] * 2,
        compiler_params=pltpu.CompilerParams(vmem_limit_bytes=32 * 2**20),
        cost_estimate=pl.CostEstimate(flops=0, bytes_accessed=rows * width * 28, transcendentals=0),
        name="join_ffn",
    )(where, *sources)


def join_attention_kernel(where_ref, *refs):
    three_ref, mix_ref = refs[-2:]
    rows = three_ref.shape[0]

    def put(ref):
        three_ref[...] = ref[:rows, :].astype(F32)
        mix_ref[...] = ref[rows:, :].astype(F32)

    pick_source(where_ref, pl.program_id(0), refs[:4], put)


def join_attention_call(where, sources, columns, inner):
    rows, cols = sources[0].shape
    return pl.pallas_call(
        join_attention_kernel,
        grid_spec=pltpu.PrefetchScalarGridSpec(
            num_scalar_prefetch=1,
            grid=(2,),
            in_specs=[
                pl.BlockSpec((rows, cols), lambda h, w, col=col: (0, col)) for col in columns
            ],
            out_specs=[
                pl.BlockSpec((rows - inner, cols), lambda h, w: (0, h)),
                pl.BlockSpec((inner, cols), lambda h, w: (0, h)),
            ],
        ),
        out_shape=[
            jax.ShapeDtypeStruct((rows - inner, 2 * cols), F32),
            jax.ShapeDtypeStruct((inner, 2 * cols), F32),
        ],
        compiler_params=pltpu.CompilerParams(vmem_limit_bytes=32 * 2**20),
        cost_estimate=pl.CostEstimate(flops=0, bytes_accessed=rows * cols * 16, transcendentals=0),
        name="join_attention",
    )(where, *sources)


def local(
    tokens, cotangent, ln_gain, ln_bias, w_qkv, b_qv, w_out, b_out, w_fc, b_fc, w_proj, b_proj
):
    core = lax.axis_index("pipe")
    place = lax.axis_index("tensor")
    line = lax.axis_index("dp")
    parts = lax.axis_size("tensor")
    dp_count = lax.axis_size("dp")
    total_rows, width = tokens.shape
    seqs = total_rows // LENGTH
    half = LENGTH // 2
    rows = seqs * half
    share = rows // parts
    piece_rows = half // parts
    inner = w_qkv.shape[3]
    hidden = w_fc.shape[2]
    first_core = core == 0

    where = jnp.stack([core, place, piece_rows]).astype(jnp.int32)
    assert seqs == 1, "one sequence"

    def both(value):
        other = swap(value, "pipe", 1)
        return jnp.where(first_core, value, other), jnp.where(first_core, other, value)

    def choose(block, value, other):
        return jnp.where(first_core == (block == 0), value, other)

    def relative(whole):
        stack = whole.reshape(seqs, 2, parts, piece_rows, width)
        mine = lax.dynamic_index_in_dim(stack, core, 1, False)
        return [
            lax.dynamic_index_in_dim(mine, place ^ m, 1, False).reshape(share, width)
            for m in range(parts)
        ]

    def widen(vec):
        return jnp.pad(vec, ((0, 0), (0, width - vec.shape[1]))) if vec.shape[1] < width else vec

    up_rows = -(-hidden // width)
    vec_rows = jnp.concatenate(
        [ln_gain[0], ln_bias[0], b_out, b_proj, b_fc.reshape(up_rows, -1), widen(b_qv[0])], axis=0
    )
    vec_both = both(vec_rows)
    qkv_other = swap(w_qkv[0], "pipe", 1)
    qkv_weights = {0: choose(0, w_qkv[0], qkv_other)}
    out_both = both(w_out[0])
    fc_other = swap(w_fc[0], "pipe", 1)
    proj_other = swap(w_proj[0], "pipe", 1)
    ffn_weights = {}

    def split_vec(vec):
        down_at = 6 + up_rows
        qv = vec[down_at : down_at + 2, :inner]
        return vec[0:2], vec[2:4], qv, vec[4], vec[6:down_at].reshape(hidden), vec[5]

    def cut(value):
        return [value[m * share : (m + 1) * share] for m in range(parts)]

    def forward(block, pieces):
        gain, shift, qv, mix_bias, up_bias, down_bias = split_vec(vec_both[block])
        w_three, w_mix = qkv_weights[block], out_both[block]
        inflow = jnp.concatenate(pieces).astype(F32)
        normed = layer_norm(inflow, gain[0], shift[0]).astype(BF)
        query = (mm(normed, w_three[0]) + qv[0]).astype(BF)
        key = mm(normed, w_three[1]).astype(BF)
        value = (mm(normed, w_three[2]) + qv[1]).astype(BF)
        pair = jnp.concatenate([key, value], axis=1)
        pair_other = swap(pair, "pipe", 1)
        mixed, log_total = attend_call(where, query, pair, pair_other)
        mix_part = mm(mixed, w_mix)
        late_fc, late_proj, late_qkv = after((fc_other, proj_other, qkv_other), mix_part)
        qkv_weights.setdefault(1, choose(1, w_qkv[0], late_qkv))
        w_up, w_down = choose(block, w_fc[0], late_fc), choose(block, w_proj[0], late_proj)
        ffn_weights[block] = (w_up, w_down)
        mix_sum = after(sum_rows(cut(mix_part)), w_up, w_down)
        residual = pieces[0].astype(F32) + mix_sum + mix_bias
        normed_two = spread_rows(layer_norm(residual, gain[1], shift[1]).astype(BF))
        pre_act = [mm(piece, w_up) + up_bias for piece in normed_two]
        gelu_out = [gelu_tanh(piece).astype(BF) for piece in pre_act]
        down_part = [mm(piece, w_down) for piece in gelu_out]
        kept = dict(
            down_part=down_part, down_bias=down_bias,
            pieces=pieces, normed=normed, query=query, pair=pair, pair_other=pair_other,
            mixed=mixed, log_total=log_total, residual=residual, normed_two=normed_two,
            pre_act=pre_act, gelu_out=gelu_out,
        )
        return kept

    def result_share(kept, down_part):
        return (kept["residual"] + sum_rows(down_part) + kept["down_bias"]).astype(BF)

    def core_sum_columns(left, right):
        size = right.shape[1] // 2
        mine = lax.dynamic_slice_in_dim(right, core * size, size, 1)
        theirs = lax.dynamic_slice_in_dim(right, (1 - core) * size, size, 1)
        sent = rows_dot(left, theirs).astype(BF)
        return (rows_dot(left, mine) + swap(sent, "pipe", 1).astype(F32)).astype(BF)

    def core_sum(left, right):
        size = left.shape[1] // 2
        mine = lax.dynamic_slice_in_dim(left, core * size, size, 1)
        theirs = lax.dynamic_slice_in_dim(left, (1 - core) * size, size, 1)
        sent = rows_dot(theirs, right).astype(BF)
        return (rows_dot(mine, right) + swap(sent, "pipe", 1).astype(F32)).astype(BF)

    def small_rows(values):
        stack = jnp.stack(values).astype(BF)
        return jnp.pad(stack, ((0, 16 - stack.shape[0]), (0, 0)))

    def backward(block, kept, grad_pieces, fillers):
        gain, shift, qv, mix_bias, up_bias, down_bias = split_vec(vec_both[block])
        w_three, w_mix = qkv_weights[block], out_both[block]
        w_up, w_down = ffn_weights[block]
        grad_share = grad_pieces[0].astype(F32)
        grad_pre = []
        for pre, piece in zip(kept["pre_act"], grad_pieces):
            grad_pre.append(jax.vjp(gelu_tanh, pre)[1](back_dot(piece, w_down))[0])
        pre_bf = [piece.astype(BF) for piece in grad_pre]
        up_part = [back_dot(piece, w_up) for piece in pre_bf]
        _, norm_two_back = jax.vjp(layer_norm, kept["residual"], gain[1], shift[1])
        g_down = core_sum(jnp.concatenate(kept["gelu_out"]), jnp.concatenate(grad_pieces))
        g_up = core_sum(jnp.concatenate(kept["normed_two"]), jnp.concatenate(pre_bf))
        grad_norm, g_gain_two, g_shift_two = norm_two_back(sum_rows(up_part))
        grad_hidden = grad_share + grad_norm
        hidden_bf = jnp.concatenate(spread_rows(grad_hidden.astype(BF)))
        hidden_bf, ffn_grads = lax.optimization_barrier((hidden_bf, fillers["ffn"](g_down, g_up)))
        middle = fillers["middle"](hidden_bf)
        g_mix = core_sum_columns(kept["mixed"], hidden_bf)
        grad_mixed = back_dot(hidden_bf, w_mix).astype(BF)
        grad_query, own_grad, other_grad = attend_back_call(
            where, kept["query"], kept["pair"], kept["pair_other"], grad_mixed, kept["log_total"]
        )
        pair_grad = own_grad + swap(other_grad, "pipe", 1).astype(F32)
        value_total = pair_grad[:, inner:]
        three_bf = jnp.concatenate([grad_query, pair_grad], axis=1).astype(BF)
        three_bf, middle = lax.optimization_barrier((three_bf, middle))
        w_flat = jnp.concatenate([w_three[0], w_three[1], w_three[2]], axis=1)
        normed_part = back_dot(three_bf, w_flat)
        normed_sum, last = lax.optimization_barrier(
            (sum_rows(cut(normed_part)), fillers["last"](middle, normed_part))
        )
        own_rows = kept["pieces"][0].astype(F32)
        _, norm_one_back = jax.vjp(layer_norm, own_rows, gain[0], shift[0])
        g_three = core_sum_columns(three_bf, kept["normed"])
        g_attention = jnp.concatenate([g_three, g_mix], axis=0)
        grad_norm_one, g_gain_one, g_shift_one = norm_one_back(normed_sum)
        grad_inflow = grad_hidden + grad_norm_one
        riders = small_rows(
            [g_gain_one, g_gain_two, g_shift_one, g_shift_two]
            + [jnp.sum(grad_hidden, axis=0), jnp.sum(grad_share, axis=0)]
        )
        gathered = spread_rows(jnp.concatenate([grad_inflow.astype(BF), riders]))
        grad_in_pieces = [piece[:share] for piece in gathered]
        shared = sum([piece[share:].astype(F32) for piece in gathered[1:]], gathered[0][share:].astype(F32))
        private_up = sum([jnp.sum(piece, axis=0) for piece in grad_pre[1:]], jnp.sum(grad_pre[0], axis=0))
        private = jnp.concatenate(
            [
                shared[:6],
                private_up.reshape(up_rows, -1),
                widen(jnp.sum(grad_query, axis=0)[None]),
                widen(jnp.sum(value_total, axis=0)[None]),
            ]
        )
        private = jnp.pad(private, ((0, 16 - private.shape[0]), (0, 0)))
        return grad_in_pieces, ffn_grads, g_attention, private, middle, last, grad_inflow

    def direct_sum(value, late):
        if dp_count != 4:
            return lax.psum(value, "dp")
        size = value.shape[0] // 4
        stack = value.reshape(4, size, value.shape[1])
        got = [
            swap(lax.dynamic_index_in_dim(stack, line ^ m, 0, False), "dp", m) for m in (1, 3, 2)
        ]
        got = lax.optimization_barrier((late, *got))[1:]
        total = lax.dynamic_index_in_dim(stack, line, 0, False).astype(F32)
        total = sum([piece.astype(F32) for piece in got], total).astype(BF)
        got = jnp.stack([total] + [swap(total, "dp", m) for m in (1, 2, 3)])
        return jnp.concatenate(
            [lax.dynamic_index_in_dim(got, line ^ j, 0, False) for j in range(4)]
        )

    def to_first(value):
        return lax.ppermute(value, "pipe", [(1, 0)])

    def to_second(value):
        return lax.ppermute(value, "pipe", [(0, 1)])

    zero_kept = forward(0, relative(tokens))
    zero_out = spread_rows(result_share(zero_kept, zero_kept["down_part"]))
    one_kept = forward(1, zero_out)
    cotangent_pieces = relative(after(cotangent, one_kept["mixed"]))
    def fill(shape, pieces):
        out = jnp.zeros(shape, BF)
        for piece, row, col in pieces:
            out = lax.dynamic_update_slice(out, piece.astype(BF), (row, col))
        return out

    one_grad, one_ffn, one_attention, one_small, one_result, _, _ = backward(
        1,
        one_kept,
        cotangent_pieces,
        dict(
            ffn=lambda down, up: fill(
                (2 * down.shape[0], width), [(down, 0, 0), (up, down.shape[0], 0)]
            ),
            middle=lambda ready: result_share(
                one_kept, [after(piece, ready) for piece in one_kept["down_part"]]
            ),
            last=lambda middle, ready: 0,
        ),
    )
    first_sum = lax.psum(one_ffn, "dp")
    zero_rows = jnp.concatenate(zero_out)
    activation_sources = lambda one_rows: (zero_rows, one_rows, to_first(zero_rows), to_second(one_rows))
    ffn_rows, ffn_half = one_ffn.shape[0], one_ffn.shape[0] // 2
    zero_grad, second, zero_attention, zero_small, _, activations, late = backward(
        0,
        zero_kept,
        one_grad,
        dict(
            ffn=lambda down, up: fill(
                (ffn_rows + 16, width + one_attention.shape[1]),
                [
                    (one_attention, 0, width),
                    (one_small, ffn_rows, 0),
                    (down, 0, 0),
                    (up, ffn_half, 0),
                ],
            ),
            middle=lambda ready: jnp.concatenate(spread_rows(after(one_result, ready))),
            last=lambda middle, ready: join_rows_call(
                where, activation_sources(after(middle, ready)), parts, BF
            ),
        ),
    )
    second, first_sum = lax.optimization_barrier((second, first_sum))
    second_sum = lax.psum(second, "dp")
    zero_attention = direct_sum(zero_attention, late)
    one_rows, zero_rows = jnp.concatenate(one_grad), jnp.concatenate(zero_grad)
    grad_inputs = join_rows_call(
        where, (zero_rows, one_rows, to_first(zero_rows), to_second(one_rows)), parts, F32
    )
    if dp_count == 4:
        zero_small = sum([swap(zero_small, "dp", m) for m in (1, 2, 3)], zero_small)
    else:
        zero_small = lax.psum(zero_small, "dp")
    zero_small = zero_small + to_first(zero_small)
    second_sum = tie(second_sum, zero_attention, grad_inputs, zero_small)
    second_got = swap(second_sum, "pipe", 1)
    g_down, g_up = join_ffn_call(
        where, (second_sum, first_sum, second_got, to_second(first_sum)), ffn_half, width
    )
    g_three, g_mix = join_attention_call(
        where,
        (zero_attention, second_sum, to_first(zero_attention), second_got),
        [0, width // zero_attention.shape[1]] * 2,
        inner,
    )
    g_three = g_three.reshape(3, inner, width).transpose(0, 2, 1)
    one_small, one_small_got = second_sum[ffn_rows:, :width], second_got[ffn_rows:, :width]
    small = jnp.where(
        first_core,
        zero_small,
        one_small.astype(F32) + one_small_got.astype(F32),
    )
    qv_at = 6 + up_rows
    return (
        activations[None],
        grad_inputs[None],
        small[None, 0:2],
        small[None, 2:4],
        g_three[None],
        small[None, qv_at : qv_at + 2, :inner],
        g_mix[None],
        small[None, 4],
        g_up[None],
        small[6:qv_at].reshape(1, hidden),
        g_down[None],
        small[None, 5],
    )


def solution(mesh):
    in_specs = (
        P("dp", None),
        P("dp", None),
        P("pipe", None, None),
        P("pipe", None, None),
        P("pipe", None, None, "tensor"),
        P("pipe", None, "tensor"),
        P("pipe", "tensor", None),
        P("pipe", None),
        P("pipe", None, "tensor"),
        P("pipe", "tensor"),
        P("pipe", "tensor", None),
        P("pipe", None),
    )
    out_specs = (
        P("pipe", "dp", None),
        P("pipe", "dp", None),
        P("pipe", None, None),
        P("pipe", None, None),
        P("pipe", None, None, "tensor"),
        P("pipe", None, "tensor"),
        P("pipe", "tensor", None),
        P("pipe", None),
        P("pipe", None, "tensor"),
        P("pipe", "tensor"),
        P("pipe", "tensor", None),
        P("pipe", None),
    )
    return jax.shard_map(local, mesh=mesh, in_specs=in_specs, out_specs=out_specs, check_vma=False)
```

```python
import jax
import jax.numpy as jnp
from jax import lax
from jax.experimental import pallas as pl
from jax.experimental.pallas import tpu as pltpu
from jax.sharding import PartitionSpec as P

HEAD_DIM = 64
LENGTH = 1024
EPSILON = 1e-05
SCALE = HEAD_DIM ** (-0.5)
BF = jnp.bfloat16
F32 = jnp.float32


def swap(value, axis, mask):
    count = lax.axis_size(axis)
    return lax.ppermute(value, axis, [(i, i ^ mask) for i in range(count)])


def layer_norm(inputs, scale_vec, shift_vec):
    centred = inputs - jnp.mean(inputs, axis=-1, keepdims=True)
    spread = jnp.mean(centred * centred, axis=-1, keepdims=True)
    return centred * lax.rsqrt(spread + EPSILON) * scale_vec + shift_vec


def gelu_tanh(inputs):
    return jax.nn.gelu(inputs, approximate=True)


def mm(left, right):
    return jnp.dot(left, right, preferred_element_type=F32)


def rows_dot(left, right):
    return lax.dot_general(left, right, (((0,), (0,)), ((), ())), preferred_element_type=F32)


def back_dot(left, right):
    return lax.dot_general(left, right, (((1,), (1,)), ((), ())), preferred_element_type=F32)


def spread_rows(share):
    return [share] + [swap(share, "tensor", m) for m in range(1, lax.axis_size("tensor"))]


def sum_rows(pieces):
    total = pieces[0].astype(F32)
    for m in range(1, len(pieces)):
        total = total + swap(pieces[m].astype(BF), "tensor", m).astype(F32)
    return total


def after(value, *earlier):
    return lax.optimization_barrier((value,) + earlier)[0]


def tie_kernel(*refs):
    del refs


def tie(value, *earlier):
    anywhere = pl.BlockSpec(memory_space=pl.ANY)
    return pl.pallas_call(
        tie_kernel,
        in_specs=[anywhere] * (1 + len(earlier)),
        out_specs=anywhere,
        out_shape=jax.ShapeDtypeStruct(value.shape, value.dtype),
        input_output_aliases={0: 0},
        name="tie",
    )(value, *earlier)


def nt_dot(left, right):
    return lax.dot_general(left, right, (((1,), (1,)), ((), ())), preferred_element_type=F32)


def key_bias(where_ref, rows):
    core, shift = where_ref[0], where_ref[1] * where_ref[2]
    keys = lax.broadcasted_iota(jnp.int32, (rows, rows), 0) ^ shift
    queries = lax.broadcasted_iota(jnp.int32, (rows, rows), 1) ^ shift
    own = jnp.where(keys <= queries, 0.0, -1e30)
    return own, jnp.where(core == 1, 0.0, -1e30)


def attend_kernel(where_ref, query_ref, own_ref, other_ref, mixed_ref, log_ref):
    rows, inner = query_ref.shape
    own_bias, other_bias = key_bias(where_ref, rows)
    own_value = own_ref[:, inner:].astype(F32).T.astype(BF)
    other_value = other_ref[:, inner:].astype(F32).T.astype(BF)
    mixed, logs = [], []
    for at in range(0, inner, HEAD_DIM):
        cols = slice(at, at + HEAD_DIM)
        query = query_ref[:, cols]
        own = nt_dot(own_ref[:, cols], query) * SCALE + own_bias
        other = nt_dot(other_ref[:, cols], query) * SCALE + other_bias
        top = jnp.maximum(
            jnp.max(own, axis=0, keepdims=True), jnp.max(other, axis=0, keepdims=True)
        )
        own, other = jnp.exp(own - top), jnp.exp(other - top)
        total = jnp.sum(own, axis=0, keepdims=True) + jnp.sum(other, axis=0, keepdims=True)
        scale = 1.0 / total
        mixed.append(
            mm(own_value[cols], (own * scale).astype(BF))
            + mm(other_value[cols], (other * scale).astype(BF))
        )
        logs.append(top + jnp.log(total))
    mixed_ref[...] = jnp.concatenate(mixed, axis=0).T.astype(BF)
    log_ref[...] = jnp.concatenate(logs, axis=0)


def attend_call(where, query, own, other):
    rows, inner = query.shape
    heads = inner // HEAD_DIM
    vmem = pl.BlockSpec(memory_space=pltpu.VMEM)
    return pl.pallas_call(
        attend_kernel,
        in_specs=[pl.BlockSpec(memory_space=pltpu.SMEM)] + [vmem] * 3,
        out_specs=[vmem] * 2,
        out_shape=[
            jax.ShapeDtypeStruct((rows, inner), BF),
            jax.ShapeDtypeStruct((heads, rows), F32),
        ],
        compiler_params=pltpu.CompilerParams(vmem_limit_bytes=40 * 2**20),
        cost_estimate=pl.CostEstimate(
            flops=8 * rows * rows * inner,
            bytes_accessed=rows * inner * 12,
            transcendentals=2 * rows * rows * heads,
        ),
        name="attend",
    )(where, query, own, other)


def attend_back_kernel(
    where_ref, query_ref, own_ref, other_ref, hidden_ref, mix_ref, log_ref,
    query_out, own_out, other_out,
):
    rows, inner = query_ref.shape
    grads = nt_dot(hidden_ref[...], mix_ref[...]).astype(BF)
    own_bias, other_bias = key_bias(where_ref, rows)
    own_key = own_ref[:, :inner].astype(F32).T.astype(BF)
    other_key = other_ref[:, :inner].astype(F32).T.astype(BF)
    grad_query = []
    for head, at in enumerate(range(0, inner, HEAD_DIM)):
        cols = slice(at, at + HEAD_DIM)
        values = slice(inner + at, inner + at + HEAD_DIM)
        query, grad = query_ref[:, cols], grads[:, cols]
        log_total = log_ref[head : head + 1, :]
        own = jnp.exp(nt_dot(own_ref[:, cols], query) * SCALE + own_bias - log_total)
        other = jnp.exp(nt_dot(other_ref[:, cols], query) * SCALE + other_bias - log_total)
        own_grad = nt_dot(own_ref[:, values], grad)
        other_grad = nt_dot(other_ref[:, values], grad)
        own_out[:, values] = mm(own.astype(BF), grad)
        other_out[:, values] = mm(other.astype(BF), grad).astype(BF)
        delta = jnp.sum(own * own_grad, axis=0, keepdims=True) + jnp.sum(
            other * other_grad, axis=0, keepdims=True
        )
        own_raw = (own * (own_grad - delta)).astype(BF)
        other_raw = (other * (other_grad - delta)).astype(BF)
        own_out[:, cols] = mm(own_raw, query) * SCALE
        other_out[:, cols] = (mm(other_raw, query) * SCALE).astype(BF)
        grad_query.append(mm(own_key[cols], own_raw) + mm(other_key[cols], other_raw))
    query_out[...] = jnp.concatenate(grad_query, axis=0).T * SCALE


def attend_back_call(where, query, own, other, hidden, w_mix, log_total):
    rows, inner = query.shape
    heads = inner // HEAD_DIM
    vmem = pl.BlockSpec(memory_space=pltpu.VMEM)
    return pl.pallas_call(
        attend_back_kernel,
        in_specs=[pl.BlockSpec(memory_space=pltpu.SMEM)] + [vmem] * 6,
        out_specs=[vmem] * 3,
        out_shape=[
            jax.ShapeDtypeStruct((rows, inner), F32),
            jax.ShapeDtypeStruct((rows, 2 * inner), F32),
            jax.ShapeDtypeStruct((rows, 2 * inner), BF),
        ],
        compiler_params=pltpu.CompilerParams(vmem_limit_bytes=40 * 2**20),
        cost_estimate=pl.CostEstimate(
            flops=20 * rows * rows * inner + 2 * hidden.size * inner,
            bytes_accessed=rows * inner * 32,
            transcendentals=2 * rows * rows * heads,
        ),
        name="attend_back",
    )(where, query, own, other, hidden, w_mix, log_total)


def pick_source(where_ref, half, refs, put):
    core = where_ref[0]
    for at, ref in enumerate(refs):
        mine = (half == core) if at < 2 else (half != core)

        @pl.when(mine & (core == at % 2))
        def _(ref=ref):
            put(ref)


def source_used(where_ref, half, at):
    core = where_ref[0]
    return ((half == core) if at < 2 else (half != core)) & (core == at % 2)


def join_rows_kernel(where_ref, *refs):
    place, half = where_ref[1], pl.program_id(0)
    out_ref = refs[-1]
    size = refs[0].shape[0] // out_ref.shape[0]

    def put(ref):
        for j in range(out_ref.shape[0]):
            rows = pl.ds(pl.multiple_of((place ^ j) * size, size), size)
            out_ref[j] = ref[rows, :].astype(out_ref.dtype)

    pick_source(where_ref, half, refs[:4], put)


def join_rows_call(where, sources, parts, dtype):
    rows, width = sources[0].shape
    size = rows // parts
    out = pl.pallas_call(
        join_rows_kernel,
        grid_spec=pltpu.PrefetchScalarGridSpec(
            num_scalar_prefetch=1,
            grid=(2,),
            in_specs=[pl.BlockSpec((rows, width), lambda h, w: (0, 0))] * 4,
            out_specs=pl.BlockSpec((parts, size, width), lambda h, w: (h, 0, 0)),
        ),
        out_shape=jax.ShapeDtypeStruct((2 * parts, size, width), dtype),
        compiler_params=pltpu.CompilerParams(vmem_limit_bytes=32 * 2**20),
        cost_estimate=pl.CostEstimate(flops=0, bytes_accessed=rows * width * 12, transcendentals=0),
        name="join_rows",
    )(where, *sources)
    return out.reshape(2 * rows, width)


def join_ffn_kernel(where_ref, *refs):
    which, half = pl.program_id(0), pl.program_id(1)
    down_ref, up_ref = refs[-2:]

    def put(ref):
        @pl.when(which == 0)
        def _():
            down_ref[...] = ref[...].astype(F32)

        @pl.when(which == 1)
        def _():
            up_ref[...] = ref[...].astype(F32)

    pick_source(where_ref, half, refs[:4], put)


def join_ffn_call(where, sources, rows, width):
    def source(at):
        return pl.BlockSpec(
            (rows, width), lambda k, h, w: (jnp.where(source_used(w, h, at) | (h == 1), k, 0), 0)
        )

    shape = jax.ShapeDtypeStruct((2 * rows, width), F32)
    return pl.pallas_call(
        join_ffn_kernel,
        grid_spec=pltpu.PrefetchScalarGridSpec(
            num_scalar_prefetch=1,
            grid=(2, 2),
            in_specs=[source(at) for at in range(4)],
            out_specs=[
                pl.BlockSpec((rows, width), lambda k, h, w: (jnp.where(k == 0, h, 1), 0)),
                pl.BlockSpec((rows, width), lambda k, h, w: (jnp.where(k == 0, 0, h), 0)),
            ],
        ),
        out_shape=[shape] * 2,
        compiler_params=pltpu.CompilerParams(vmem_limit_bytes=32 * 2**20),
        cost_estimate=pl.CostEstimate(flops=0, bytes_accessed=rows * width * 28, transcendentals=0),
        name="join_ffn",
    )(where, *sources)


def join_attention_kernel(where_ref, *refs):
    three_ref, mix_ref = refs[-2:]
    rows = three_ref.shape[0]

    def put(ref):
        three_ref[...] = ref[:rows, :].astype(F32)
        mix_ref[...] = ref[rows:, :].astype(F32)

    pick_source(where_ref, pl.program_id(0), refs[:4], put)


def join_attention_call(where, sources, columns, inner):
    rows, cols = sources[0].shape
    return pl.pallas_call(
        join_attention_kernel,
        grid_spec=pltpu.PrefetchScalarGridSpec(
            num_scalar_prefetch=1,
            grid=(2,),
            in_specs=[
                pl.BlockSpec((rows, cols), lambda h, w, col=col: (0, col)) for col in columns
            ],
            out_specs=[
                pl.BlockSpec((rows - inner, cols), lambda h, w: (0, h)),
                pl.BlockSpec((inner, cols), lambda h, w: (0, h)),
            ],
        ),
        out_shape=[
            jax.ShapeDtypeStruct((rows - inner, 2 * cols), F32),
            jax.ShapeDtypeStruct((inner, 2 * cols), F32),
        ],
        compiler_params=pltpu.CompilerParams(vmem_limit_bytes=32 * 2**20),
        cost_estimate=pl.CostEstimate(flops=0, bytes_accessed=rows * cols * 16, transcendentals=0),
        name="join_attention",
    )(where, *sources)


def local(
    tokens, cotangent, ln_gain, ln_bias, w_qkv, b_qv, w_out, b_out, w_fc, b_fc, w_proj, b_proj
):
    core = lax.axis_index("pipe")
    place = lax.axis_index("tensor")
    line = lax.axis_index("dp")
    parts = lax.axis_size("tensor")
    dp_count = lax.axis_size("dp")
    total_rows, width = tokens.shape
    seqs = total_rows // LENGTH
    half = LENGTH // 2
    rows = seqs * half
    share = rows // parts
    piece_rows = half // parts
    inner = w_qkv.shape[3]
    hidden = w_fc.shape[2]
    first_core = core == 0

    where = jnp.stack([core, place, piece_rows]).astype(jnp.int32)
    assert seqs == 1, "one sequence"

    def both(value):
        other = swap(value, "pipe", 1)
        return jnp.where(first_core, value, other), jnp.where(first_core, other, value)

    def choose(block, value, other):
        return jnp.where(first_core == (block == 0), value, other)

    def relative(whole):
        stack = whole.reshape(seqs, 2, parts, piece_rows, width)
        mine = lax.dynamic_index_in_dim(stack, core, 1, False)
        return [
            lax.dynamic_index_in_dim(mine, place ^ m, 1, False).reshape(share, width)
            for m in range(parts)
        ]

    def widen(vec):
        return jnp.pad(vec, ((0, 0), (0, width - vec.shape[1]))) if vec.shape[1] < width else vec

    up_rows = -(-hidden // width)
    vec_rows = jnp.concatenate(
        [ln_gain[0], ln_bias[0], b_out, b_proj, b_fc.reshape(up_rows, -1), widen(b_qv[0])], axis=0
    )
    vec_both = both(vec_rows)
    qkv_other = swap(w_qkv[0], "pipe", 1)
    qkv_weights = {0: choose(0, w_qkv[0], qkv_other)}
    out_both = both(w_out[0])
    fc_other = swap(w_fc[0], "pipe", 1)
    proj_other = swap(w_proj[0], "pipe", 1)
    ffn_weights = {}

    def split_vec(vec):
        down_at = 6 + up_rows
        qv = vec[down_at : down_at + 2, :inner]
        return vec[0:2], vec[2:4], qv, vec[4], vec[6:down_at].reshape(hidden), vec[5]

    def cut(value):
        return [value[m * share : (m + 1) * share] for m in range(parts)]

    def forward(block, pieces):
        gain, shift, qv, mix_bias, up_bias, down_bias = split_vec(vec_both[block])
        w_three, w_mix = qkv_weights[block], out_both[block]
        inflow = jnp.concatenate(pieces).astype(F32)
        normed = layer_norm(inflow, gain[0], shift[0]).astype(BF)
        query = (mm(normed, w_three[0]) + qv[0]).astype(BF)
        key = mm(normed, w_three[1]).astype(BF)
        value = (mm(normed, w_three[2]) + qv[1]).astype(BF)
        pair = jnp.concatenate([key, value], axis=1)
        pair_other = swap(pair, "pipe", 1)
        mixed, log_total = attend_call(where, query, pair, pair_other)
        mix_part = mm(mixed, w_mix)
        late_fc, late_proj, late_qkv = after((fc_other, proj_other, qkv_other), mix_part)
        qkv_weights.setdefault(1, choose(1, w_qkv[0], late_qkv))
        w_up, w_down = choose(block, w_fc[0], late_fc), choose(block, w_proj[0], late_proj)
        ffn_weights[block] = (w_up, w_down)
        mix_sum = after(sum_rows(cut(mix_part)), w_up, w_down)
        residual = pieces[0].astype(F32) + mix_sum + mix_bias
        normed_two = spread_rows(layer_norm(residual, gain[1], shift[1]).astype(BF))
        pre_act = [mm(piece, w_up) + up_bias for piece in normed_two]
        gelu_out = [gelu_tanh(piece).astype(BF) for piece in pre_act]
        down_part = [mm(piece, w_down) for piece in gelu_out]
        kept = dict(
            down_part=down_part, down_bias=down_bias,
            pieces=pieces, normed=normed, query=query, pair=pair, pair_other=pair_other,
            mixed=mixed, log_total=log_total, residual=residual, normed_two=normed_two,
            pre_act=pre_act, gelu_out=gelu_out,
        )
        return kept

    def result_share(kept, down_part):
        return (kept["residual"] + sum_rows(down_part) + kept["down_bias"]).astype(BF)

    def core_sum_columns(left, right):
        size = right.shape[1] // 2
        mine = lax.dynamic_slice_in_dim(right, core * size, size, 1)
        theirs = lax.dynamic_slice_in_dim(right, (1 - core) * size, size, 1)
        sent = rows_dot(left, theirs).astype(BF)
        return (rows_dot(left, mine) + swap(sent, "pipe", 1).astype(F32)).astype(BF)

    def core_sum(left, right):
        size = left.shape[1] // 2
        mine = lax.dynamic_slice_in_dim(left, core * size, size, 1)
        theirs = lax.dynamic_slice_in_dim(left, (1 - core) * size, size, 1)
        sent = rows_dot(theirs, right).astype(BF)
        return (rows_dot(mine, right) + swap(sent, "pipe", 1).astype(F32)).astype(BF)

    def small_rows(values):
        stack = jnp.stack(values).astype(BF)
        return jnp.pad(stack, ((0, 16 - stack.shape[0]), (0, 0)))

    def backward(block, kept, grad_pieces, fillers):
        gain, shift, qv, mix_bias, up_bias, down_bias = split_vec(vec_both[block])
        w_three, w_mix = qkv_weights[block], out_both[block]
        w_up, w_down = ffn_weights[block]
        grad_share = grad_pieces[0].astype(F32)
        grad_pre = []
        for pre, piece in zip(kept["pre_act"], grad_pieces):
            grad_pre.append(jax.vjp(gelu_tanh, pre)[1](back_dot(piece, w_down))[0])
        pre_bf = [piece.astype(BF) for piece in grad_pre]
        up_part = [back_dot(piece, w_up) for piece in pre_bf]
        _, norm_two_back = jax.vjp(layer_norm, kept["residual"], gain[1], shift[1])
        g_down = core_sum(jnp.concatenate(kept["gelu_out"]), jnp.concatenate(grad_pieces))
        g_up = core_sum(jnp.concatenate(kept["normed_two"]), jnp.concatenate(pre_bf))
        grad_norm, g_gain_two, g_shift_two = norm_two_back(sum_rows(up_part))
        grad_hidden = grad_share + grad_norm
        hidden_bf = jnp.concatenate(spread_rows(grad_hidden.astype(BF)))
        hidden_bf, ffn_grads = lax.optimization_barrier((hidden_bf, fillers["ffn"](g_down, g_up)))
        middle = fillers["middle"](hidden_bf)
        g_mix = core_sum_columns(kept["mixed"], hidden_bf)
        grad_query, own_grad, other_grad = attend_back_call(
            where, kept["query"], kept["pair"], kept["pair_other"], hidden_bf, w_mix, kept["log_total"]
        )
        pair_grad = own_grad + swap(other_grad, "pipe", 1).astype(F32)
        value_total = pair_grad[:, inner:]
        three_bf = jnp.concatenate([grad_query, pair_grad], axis=1).astype(BF)
        three_bf, middle = lax.optimization_barrier((three_bf, middle))
        w_flat = jnp.concatenate([w_three[0], w_three[1], w_three[2]], axis=1)
        normed_part = back_dot(three_bf, w_flat)
        normed_sum, last = lax.optimization_barrier(
            (sum_rows(cut(normed_part)), fillers["last"](middle, normed_part))
        )
        own_rows = kept["pieces"][0].astype(F32)
        _, norm_one_back = jax.vjp(layer_norm, own_rows, gain[0], shift[0])
        g_three = core_sum_columns(three_bf, kept["normed"])
        g_attention = jnp.concatenate([g_three, g_mix], axis=0)
        grad_norm_one, g_gain_one, g_shift_one = norm_one_back(normed_sum)
        grad_inflow = grad_hidden + grad_norm_one
        riders = small_rows(
            [g_gain_one, g_gain_two, g_shift_one, g_shift_two]
            + [jnp.sum(grad_hidden, axis=0), jnp.sum(grad_share, axis=0)]
        )
        gathered = spread_rows(jnp.concatenate([grad_inflow.astype(BF), riders]))
        grad_in_pieces = [piece[:share] for piece in gathered]
        shared = sum([piece[share:].astype(F32) for piece in gathered[1:]], gathered[0][share:].astype(F32))
        private_up = sum([jnp.sum(piece, axis=0) for piece in grad_pre[1:]], jnp.sum(grad_pre[0], axis=0))
        private = jnp.concatenate(
            [
                shared[:6],
                private_up.reshape(up_rows, -1),
                widen(jnp.sum(grad_query, axis=0)[None]),
                widen(jnp.sum(value_total, axis=0)[None]),
            ]
        )
        private = jnp.pad(private, ((0, 16 - private.shape[0]), (0, 0)))
        return grad_in_pieces, ffn_grads, g_attention, private, middle, last, grad_inflow

    def direct_sum(value, late):
        if dp_count != 4:
            return lax.psum(value, "dp")
        size = value.shape[0] // 4
        stack = value.reshape(4, size, value.shape[1])
        got = [
            swap(lax.dynamic_index_in_dim(stack, line ^ m, 0, False), "dp", m) for m in (1, 3, 2)
        ]
        got = lax.optimization_barrier((late, *got))[1:]
        total = lax.dynamic_index_in_dim(stack, line, 0, False).astype(F32)
        total = sum([piece.astype(F32) for piece in got], total).astype(BF)
        got = jnp.stack([total] + [swap(total, "dp", m) for m in (1, 2, 3)])
        return jnp.concatenate(
            [lax.dynamic_index_in_dim(got, line ^ j, 0, False) for j in range(4)]
        )

    def to_first(value):
        return lax.ppermute(value, "pipe", [(1, 0)])

    def to_second(value):
        return lax.ppermute(value, "pipe", [(0, 1)])

    zero_kept = forward(0, relative(tokens))
    zero_out = spread_rows(result_share(zero_kept, zero_kept["down_part"]))
    one_kept = forward(1, zero_out)
    cotangent_pieces = relative(after(cotangent, one_kept["mixed"]))
    def fill(shape, pieces):
        out = jnp.zeros(shape, BF)
        for piece, row, col in pieces:
            out = lax.dynamic_update_slice(out, piece.astype(BF), (row, col))
        return out

    one_grad, one_ffn, one_attention, one_small, one_result, _, _ = backward(
        1,
        one_kept,
        cotangent_pieces,
        dict(
            ffn=lambda down, up: fill(
                (2 * down.shape[0], width), [(down, 0, 0), (up, down.shape[0], 0)]
            ),
            middle=lambda ready: result_share(
                one_kept, [after(piece, ready) for piece in one_kept["down_part"]]
            ),
            last=lambda middle, ready: 0,
        ),
    )
    first_sum = lax.psum(one_ffn, "dp")
    zero_rows = jnp.concatenate(zero_out)
    activation_sources = lambda one_rows: (zero_rows, one_rows, to_first(zero_rows), to_second(one_rows))
    ffn_rows, ffn_half = one_ffn.shape[0], one_ffn.shape[0] // 2
    zero_grad, second, zero_attention, zero_small, _, activations, late = backward(
        0,
        zero_kept,
        one_grad,
        dict(
            ffn=lambda down, up: fill(
                (ffn_rows + 16, width + one_attention.shape[1]),
                [
                    (one_attention, 0, width),
                    (one_small, ffn_rows, 0),
                    (down, 0, 0),
                    (up, ffn_half, 0),
                ],
            ),
            middle=lambda ready: jnp.concatenate(spread_rows(after(one_result, ready))),
            last=lambda middle, ready: join_rows_call(
                where, activation_sources(after(middle, ready)), parts, BF
            ),
        ),
    )
    second, first_sum = lax.optimization_barrier((second, first_sum))
    second_sum = lax.psum(second, "dp")
    zero_attention = direct_sum(zero_attention, late)
    one_rows, zero_rows = jnp.concatenate(one_grad), jnp.concatenate(zero_grad)
    grad_inputs = join_rows_call(
        where, (zero_rows, one_rows, to_first(zero_rows), to_second(one_rows)), parts, F32
    )
    if dp_count == 4:
        zero_small = sum([swap(zero_small, "dp", m) for m in (1, 2, 3)], zero_small)
    else:
        zero_small = lax.psum(zero_small, "dp")
    zero_small = zero_small + to_first(zero_small)
    second_sum = tie(second_sum, zero_attention, grad_inputs, zero_small)
    second_got = swap(second_sum, "pipe", 1)
    g_down, g_up = join_ffn_call(
        where, (second_sum, first_sum, second_got, to_second(first_sum)), ffn_half, width
    )
    g_three, g_mix = join_attention_call(
        where,
        (zero_attention, second_sum, to_first(zero_attention), second_got),
        [0, width // zero_attention.shape[1]] * 2,
        inner,
    )
    g_three = g_three.reshape(3, inner, width).transpose(0, 2, 1)
    one_small, one_small_got = second_sum[ffn_rows:, :width], second_got[ffn_rows:, :width]
    small = jnp.where(
        first_core,
        zero_small,
        one_small.astype(F32) + one_small_got.astype(F32),
    )
    qv_at = 6 + up_rows
    return (
        activations[None],
        grad_inputs[None],
        small[None, 0:2],
        small[None, 2:4],
        g_three[None],
        small[None, qv_at : qv_at + 2, :inner],
        g_mix[None],
        small[None, 4],
        g_up[None],
        small[6:qv_at].reshape(1, hidden),
        g_down[None],
        small[None, 5],
    )


def solution(mesh):
    in_specs = (
        P("dp", None),
        P("dp", None),
        P("pipe", None, None),
        P("pipe", None, None),
        P("pipe", None, None, "tensor"),
        P("pipe", None, "tensor"),
        P("pipe", "tensor", None),
        P("pipe", None),
        P("pipe", None, "tensor"),
        P("pipe", "tensor"),
        P("pipe", "tensor", None),
        P("pipe", None),
    )
    out_specs = (
        P("pipe", "dp", None),
        P("pipe", "dp", None),
        P("pipe", None, None),
        P("pipe", None, None),
        P("pipe", None, None, "tensor"),
        P("pipe", None, "tensor"),
        P("pipe", "tensor", None),
        P("pipe", None),
        P("pipe", None, "tensor"),
        P("pipe", "tensor"),
        P("pipe", "tensor", None),
        P("pipe", None),
    )
    return jax.shard_map(local, mesh=mesh, in_specs=in_specs, out_specs=out_specs, check_vma=False)
```
